32 devices in a mesh: row: 16 (over z, x, core), col: 2 (over y).
Axes of the slice: x: 2, y: 2, z: 4, core: 2. Of those that a mesh axis runs over, the one named last changes fastest.
Arguments:
- matrix: float32 [4096, 1024], P('row', 'col'), may hold values from -12 to 12
Outputs:
- rotated: float32 [4096, 1024], P('row', 'col')
- coupling: float32 [2], replicated
The draws below stay inside these ranges and needn't reach their ends.
All inputs are finite; a program needn't handle non-finite values.
Results may differ from the reference program's by a relative error of at most 0.00027.
Values sent between devices are 32-bit elements; how exact they have to be, the bound alone decides.
A program may use at most 64 MiB of HBM per device.

```python
import math
import jax
import jax.numpy as jnp
from jax import lax

BW = 256
STEPS = 2
NB = 4
ROWS = 4096


def draw_matrix(key, part):
    subkeys = jax.random.split(key, 4)
    column_index = jnp.arange(NB * BW, dtype=jnp.float32)[None, :] / (NB * BW)
    rising = jnp.exp(math.log(1.6) * column_index)
    spread = jnp.exp(jax.random.uniform(subkeys[0], (1, NB * BW), jnp.float32, 0.0, math.log(2.5)))
    loading = jax.random.uniform(subkeys[1], (1, NB * BW), jnp.float32, -1.0, 1.0) * (0.5 + column_index)
    common = jnp.clip(jax.random.normal(subkeys[2], (ROWS, 1), jnp.float32), -4.0, 4.0)
    noise_part = jax.random.normal(subkeys[3], (ROWS, NB * BW), jnp.float32)
    strength = 0.3
    combined = noise_part + 0.4 * jnp.roll(noise_part, 1, axis=1) + strength * common * loading
    return jnp.clip(combined * spread * rising, -12.0, 12.0)


def setup_inputs(seed: int = 0) -> dict:
    keys = jax.random.split(jax.random.key(seed), 2)
    matrix = draw_matrix(jax.random.fold_in(keys[1], 71), 0)
    return {"matrix": matrix}


def pair_rotation(pair_gram):
    lower_factor = jnp.linalg.cholesky(pair_gram)
    inner_gram = jnp.dot(lower_factor.T, lower_factor, precision=lax.Precision.HIGHEST)
    second = jnp.linalg.cholesky(inner_gram)
    return jax.scipy.linalg.solve_triangular(second, lower_factor.T, lower=True).T

def one_pair(blocks_pair):
    top_block, bottom_block = blocks_pair
    joined = jnp.concatenate([top_block, bottom_block], axis=1)
    pair_gram = jnp.dot(joined.T, joined, precision=lax.Precision.HIGHEST)
    diagonal = jnp.diagonal(pair_gram)
    cross = pair_gram[:BW, BW:]
    term = jnp.sum(cross * cross / (diagonal[:BW, None] * diagonal[None, BW:]))
    turned = jnp.dot(joined, pair_rotation(pair_gram), precision=lax.Precision.HIGHEST)
    return (turned[:, :BW], turned[:, BW:], term)

def reference(matrix):
    slots = NB // 2
    blocks = matrix.reshape(ROWS, slots, 2, BW)
    top_blocks = jnp.transpose(blocks[:, :, 0], (1, 0, 2))
    bottom_blocks = jnp.transpose(blocks[:, :, 1], (1, 0, 2))
    totals = []
    for step_index in range(STEPS):
        top_new, bottom_new, terms = lax.map(one_pair, (top_blocks, bottom_blocks))
        totals.append(jnp.sum(terms))
        top_blocks = jnp.concatenate([top_new[0:1], bottom_new[0:1], top_new[1:slots - 1]], axis=0)
        bottom_blocks = jnp.concatenate([bottom_new[1:], top_new[slots - 1:]], axis=0)
    coupling = jnp.sqrt(jnp.stack(totals) / (NB * BW // 2))
    stacked = jnp.stack([top_blocks, bottom_blocks], axis=1)
    rotated = jnp.transpose(stacked, (2, 0, 1, 3)).reshape(ROWS, NB * BW)
    return (rotated, coupling)
```

```python
import jax
import jax.numpy as jnp
from jax import lax
from jax.experimental import pallas as pl
from jax.experimental.pallas import tpu as pltpu
from jax.sharding import PartitionSpec as P

STEPS = 2


def from_behind(value, axis, steps):
    count = lax.axis_size(axis)
    first, last = (max(0, -steps), min(count, count - steps))
    return lax.ppermute(value, axis, [(source, source + steps) for source in range(first, last)])


def pair_grams(pair_blocks):
    return jnp.einsum(
        "prk,prl->pkl",
        pair_blocks,
        pair_blocks,
        precision=lax.Precision.HIGHEST,
        preferred_element_type=jnp.float32,
    )


LEAF = 128
GROUP = 8
AHEAD = 4


def mat(left, right, contract):
    return lax.dot_general(
        left,
        right,
        (contract, ((), ())),
        precision=lax.Precision.HIGHEST,
        preferred_element_type=jnp.float32,
    )


def spread(row, shape):
    return jnp.broadcast_to(row, shape)


def inverse_factors(blocks):
    shape = (GROUP, LEAF)
    groups = LEAF // GROUP
    lane = lax.broadcasted_iota(jnp.int32, shape, 1)
    sub = lax.broadcasted_iota(jnp.int32, shape, 0)
    works = [[block[GROUP * i : GROUP * (i + 1), :] for i in range(groups)] for block in blocks]
    for start in range(0, LEAF, AHEAD):
        first = start // GROUP
        columns = [
            [
                [spread(work[i][:, start + t : start + t + 1], shape) for i in range(first, groups)]
                for t in range(AHEAD)
            ]
            for work in works
        ]
        for t in range(AHEAD):
            pivot = start + t
            inside = pivot % GROUP
            for work, column in zip(works, columns):
                own = column[t]
                scale = 1.0 / spread(own[0][inside : inside + 1, :], shape)
                for later in range(t + 1, AHEAD):
                    place = inside + later - t
                    factor = spread(own[0][place : place + 1, :], shape) * scale
                    column[later] = [c - o * factor for c, o in zip(column[later], own)]
                row = spread(work[first][inside : inside + 1, :], shape)
                here = lane == pivot
                row = jnp.where(here, 1.0, row) * scale
                for i in range(first, groups):
                    held = work[i]
                    if i == first:
                        below = sub > inside
                        updated = jnp.where(here, 0.0, held) - own[0] * row
                        work[i] = jnp.where(below, updated, held)
                    else:
                        work[i] = jnp.where(here, 0.0, held) - own[i - first] * row
    results = []
    for work in works:
        full = jnp.concatenate(work, axis=0)
        rows = lax.broadcasted_iota(jnp.int32, full.shape, 0)
        lanes = lax.broadcasted_iota(jnp.int32, full.shape, 1)
        pivots = jnp.sum(jnp.where(rows == lanes, full, 0.0), axis=1, keepdims=True)
        unit = jnp.where(rows == lanes, 1.0, jnp.where(rows > lanes, full, 0.0))
        results.append(unit * lax.rsqrt(pivots))
    return results


def rotation_kernel(gram_ref, turn_ref, term_ref, work, part, inner):
    size = gram_ref.shape[0]
    half = size // 2
    count = size // LEAF
    gram = gram_ref[...]
    rows = lax.broadcasted_iota(jnp.int32, (size, size), 0)
    lanes = lax.broadcasted_iota(jnp.int32, (size, size), 1)
    diagonal = jnp.where(rows == lanes, gram, 0.0)
    down = jnp.sum(diagonal, axis=1, keepdims=True)[:half]
    across = jnp.sum(diagonal, axis=0, keepdims=True)[:, half:]
    cross = gram[:half, half:]
    total = jnp.sum(cross * cross / (down * across), axis=1, keepdims=True)
    total = jnp.sum(total, axis=0, keepdims=True)
    term_ref[...] = jnp.broadcast_to(total, term_ref.shape)

    eye = (
        lax.broadcasted_iota(jnp.int32, (LEAF, LEAF), 0)
        == lax.broadcasted_iota(jnp.int32, (LEAF, LEAF), 1)
    ).astype(jnp.float32)
    work[...] = gram
    turn_ref[...] = jnp.zeros_like(turn_ref)
    inner[...] = eye
    place_lanes = lax.broadcasted_iota(jnp.int32, (LEAF, size), 1)

    def stage(index, carry):
        now = jnp.minimum(index, count - 1)
        here = pl.ds(pl.multiple_of(now * LEAF, LEAF), LEAF)
        outer_inverse, inner_inverse = inverse_factors([work[here, here], inner[...]])

        @pl.when(index > 0)
        def _():
            before = pl.ds(pl.multiple_of((index - 1) * LEAF, LEAF), LEAF)
            turn_ref[before, :] = mat(inner_inverse, part[...], ((1,), (0,)))

        @pl.when(index < count)
        def _():
            factor = mat(outer_inverse, work[here, :], ((1,), (0,)))
            factor = jnp.where(place_lanes >= now * LEAF, factor, 0.0)
            turned = turn_ref[...]
            overlap = mat(factor, turned, ((1,), (1,)))
            rest = factor - mat(overlap, turned, ((1,), (0,)))
            part[...] = rest
            inner[...] = mat(rest, rest, ((1,), (1,)))
            work[...] -= mat(factor, factor, ((0,), (0,)))

        return carry

    lax.fori_loop(0, count + 1, stage, 0)


def rotation_of(pair_gram):
    size = pair_gram.shape[0]
    vmem = pl.BlockSpec(memory_space=pltpu.VMEM)
    turn, term = pl.pallas_call(
        rotation_kernel,
        out_shape=(
            jax.ShapeDtypeStruct((size, size), jnp.float32),
            jax.ShapeDtypeStruct((8, 128), jnp.float32),
        ),
        in_specs=[vmem],
        out_specs=(vmem, vmem),
        scratch_shapes=[
            pltpu.VMEM((size, size), jnp.float32),
            pltpu.VMEM((LEAF, size), jnp.float32),
            pltpu.VMEM((LEAF, LEAF), jnp.float32),
        ],
        compiler_params=pltpu.CompilerParams(vmem_limit_bytes=32 << 20),
    )(pair_gram)
    return turn, term[0, 0]


def body(matrix):
    width = matrix.shape[1] // 2
    col_place = lax.axis_index("col")
    col_last = lax.axis_size("col") - 1
    first_col = col_place == 0
    last_col = col_place == col_last
    top_block = matrix[:, :width]
    bottom_block = matrix[:, width:]
    pair_blocks = matrix[None]
    pair_gram = lax.psum(pair_grams(pair_blocks), "row")
    coupling_terms = []
    for step_index in range(STEPS):
        turn, local_term = rotation_of(pair_gram[0])
        coupling_terms.append(local_term)
        turned = jnp.einsum(
            "prk,lk->prl",
            pair_blocks,
            turn,
            precision=lax.Precision.HIGHEST,
            preferred_element_type=jnp.float32,
        )
        new_top = turned[0, :, :width]
        new_bottom = turned[0, :, width:]
        outgoing = jnp.where(first_col, new_bottom, new_top)
        arrived_top = from_behind(outgoing, "col", 1)
        arrived_bottom = from_behind(new_bottom, "col", -1)
        top_block = jnp.where(first_col, new_top, arrived_top)
        bottom_block = jnp.where(last_col, new_top, arrived_bottom)
        pair_blocks = jnp.concatenate([top_block, bottom_block], axis=1)[None]
        if step_index + 1 < STEPS:
            pair_gram = lax.psum(pair_grams(pair_blocks), "row")
    totals = lax.psum(jnp.stack(coupling_terms), "col")
    coupling = jnp.sqrt(totals / (1.0 * lax.axis_size("col") * width))
    rotated = jnp.concatenate([top_block, bottom_block], axis=1)
    return (rotated, coupling)


def solution(mesh):
    in_specs = (P("row", "col"),)
    out_specs = (P("row", "col"), P())
    return jax.shard_map(body, mesh=mesh, in_specs=in_specs, out_specs=out_specs, check_vma=False)
```

```python
import functools

import jax
import jax.numpy as jnp
from jax import lax
from jax.experimental import pallas as pl
from jax.experimental.pallas import tpu as pltpu
from jax.sharding import PartitionSpec as P

STEPS = 2


def from_behind(value, axis, steps):
    count = lax.axis_size(axis)
    first, last = (max(0, -steps), min(count, count - steps))
    return lax.ppermute(value, axis, [(source, source + steps) for source in range(first, last)])


LEAF = 128
GROUP = 8
AHEAD = 4


def mat(left, right, contract):
    return lax.dot_general(
        left,
        right,
        (contract, ((), ())),
        precision=lax.Precision.HIGHEST,
        preferred_element_type=jnp.float32,
    )


def spread(row, shape):
    return jnp.broadcast_to(row, shape)


def inverse_factors(blocks):
    shape = (GROUP, LEAF)
    groups = LEAF // GROUP
    lane = lax.broadcasted_iota(jnp.int32, shape, 1)
    sub = lax.broadcasted_iota(jnp.int32, shape, 0)
    works = [[block[GROUP * i : GROUP * (i + 1), :] for i in range(groups)] for block in blocks]
    for start in range(0, LEAF, AHEAD):
        first = start // GROUP
        columns = [
            [
                [spread(work[i][:, start + t : start + t + 1], shape) for i in range(first, groups)]
                for t in range(AHEAD)
            ]
            for work in works
        ]
        for t in range(AHEAD):
            pivot = start + t
            inside = pivot % GROUP
            for work, column in zip(works, columns):
                own = column[t]
                scale = 1.0 / spread(own[0][inside : inside + 1, :], shape)
                for later in range(t + 1, AHEAD):
                    place = inside + later - t
                    factor = spread(own[0][place : place + 1, :], shape) * scale
                    column[later] = [c - o * factor for c, o in zip(column[later], own)]
                row = spread(work[first][inside : inside + 1, :], shape)
                here = lane == pivot
                row = jnp.where(here, 1.0, row) * scale
                for i in range(first, groups):
                    held = work[i]
                    if i == first:
                        below = sub > inside
                        updated = jnp.where(here, 0.0, held) - own[0] * row
                        work[i] = jnp.where(below, updated, held)
                    else:
                        work[i] = jnp.where(here, 0.0, held) - own[i - first] * row
    results = []
    for work in works:
        full = jnp.concatenate(work, axis=0)
        rows = lax.broadcasted_iota(jnp.int32, full.shape, 0)
        lanes = lax.broadcasted_iota(jnp.int32, full.shape, 1)
        pivots = jnp.sum(jnp.where(rows == lanes, full, 0.0), axis=1, keepdims=True)
        unit = jnp.where(rows == lanes, 1.0, jnp.where(rows > lanes, full, 0.0))
        results.append(unit * lax.rsqrt(pivots))
    return results


def rotation_kernel(gram_ref, turn_ref, term_ref, work, part, inner):
    half = gram_ref.shape[1]
    size = 2 * half
    count = size // LEAF
    same = lax.broadcasted_iota(jnp.int32, (half, half), 0) == lax.broadcasted_iota(
        jnp.int32, (half, half), 1
    )
    top, cross, bottom = (gram_ref[half * i : half * (i + 1), :] for i in range(3))
    down = jnp.sum(jnp.where(same, top, 0.0), axis=1, keepdims=True)
    across = jnp.sum(jnp.where(same, bottom, 0.0), axis=0, keepdims=True)
    total = jnp.sum(cross * cross / (down * across), axis=1, keepdims=True)
    total = jnp.sum(total, axis=0, keepdims=True)
    term_ref[...] = jnp.broadcast_to(total, term_ref.shape)

    eye = (
        lax.broadcasted_iota(jnp.int32, (LEAF, LEAF), 0)
        == lax.broadcasted_iota(jnp.int32, (LEAF, LEAF), 1)
    ).astype(jnp.float32)
    work[:half, :half] = top
    work[:half, half:] = cross
    work[half:, :half] = jnp.zeros_like(cross)
    work[half:, half:] = bottom
    turn_ref[...] = jnp.zeros_like(turn_ref)
    inner[...] = eye
    place_lanes = lax.broadcasted_iota(jnp.int32, (LEAF, size), 1)

    def stage(index, carry):
        now = jnp.minimum(index, count - 1)
        here = pl.ds(pl.multiple_of(now * LEAF, LEAF), LEAF)
        outer_inverse, inner_inverse = inverse_factors([work[here, here], inner[...]])

        @pl.when(index > 0)
        def _():
            before = pl.ds(pl.multiple_of((index - 1) * LEAF, LEAF), LEAF)
            turn_ref[before, :] = mat(inner_inverse, part[...], ((1,), (0,)))

        @pl.when(index < count)
        def _():
            factor = mat(outer_inverse, work[here, :], ((1,), (0,)))
            factor = jnp.where(place_lanes >= now * LEAF, factor, 0.0)
            turned = turn_ref[...]
            overlap = mat(factor, turned, ((1,), (1,)))
            rest = factor - mat(overlap, turned, ((1,), (0,)))
            part[...] = rest
            inner[...] = mat(rest, rest, ((1,), (1,)))
            work[...] -= mat(factor, factor, ((0,), (0,)))

        return carry

    lax.fori_loop(0, count + 1, stage, 0)


def rotation_of(pair_gram):
    size = 2 * pair_gram.shape[1]
    vmem = pl.BlockSpec(memory_space=pltpu.VMEM)
    turn, term = pl.pallas_call(
        rotation_kernel,
        out_shape=(
            jax.ShapeDtypeStruct((size, size), jnp.float32),
            jax.ShapeDtypeStruct((8, 128), jnp.float32),
        ),
        in_specs=[vmem],
        out_specs=(vmem, vmem),
        scratch_shapes=[
            pltpu.VMEM((size, size), jnp.float32),
            pltpu.VMEM((LEAF, size), jnp.float32),
            pltpu.VMEM((LEAF, LEAF), jnp.float32),
        ],
        compiler_params=pltpu.CompilerParams(vmem_limit_bytes=32 << 20),
    )(pair_gram)
    return turn, term[0, 0]


def reduce_kernel(count, pair_ref, out_ref, mine, half_in, half, part_in, part, chunk_in, send, recv):
    width = pair_ref.shape[1] // 2
    rows = out_ref.shape[0]
    planes = count // 4
    place = lax.axis_index("row")
    core = lax.rem(place, 2)
    side = lax.rem(place // 2, 2)
    plane = place // 4
    other_core = place + 1 - 2 * core
    other_side = place + 2 - 4 * side
    others = [4 * lax.rem(plane + step, planes) + 2 * side + core for step in range(1, planes)]

    barrier = pltpu.get_barrier_semaphore()
    for peer in [other_core, other_side] + others:
        pl.semaphore_signal(
            barrier, inc=1, device_id={"row": peer}, device_id_type=pl.DeviceIdType.MESH
        )

    top = pair_ref[:, :width]
    bottom = pair_ref[:, width:]
    mine[:width, :] = mat(top, top, ((0,), (0,)))
    mine[width : 2 * width, :] = mat(top, bottom, ((0,), (0,)))
    mine[2 * width :, :] = mat(bottom, bottom, ((0,), (0,)))
    pl.semaphore_wait(barrier, 1 + planes)

    def put(source, target, index, peer):
        copy = pltpu.make_async_remote_copy(
            src_ref=source,
            dst_ref=target,
            send_sem=send.at[index],
            recv_sem=recv.at[index],
            device_id={"row": peer},
            device_id_type=pl.DeviceIdType.MESH,
        )
        copy.start()
        return copy

    def span(start, length):
        return pl.ds(pl.multiple_of(start, 8), length)

    large, middle, small = rows // 2, rows // 4, rows // count
    put(mine.at[span((1 - core) * large, large)], half_in, 0, other_core).wait()
    half[...] = mine[span(core * large, large), :] + half_in[...]
    put(half.at[span((1 - side) * middle, middle)], part_in, 1, other_side).wait()
    part[...] = half[span(side * middle, middle), :] + part_in[...]
    copies = []
    for step in range(1, planes):
        there = lax.rem(plane + step, planes)
        source = part.at[span(there * small, small)]
        copies.append(put(source, chunk_in.at[step - 1], 1 + step, others[step - 1]))
    total = part[span(plane * small, small), :]
    for step in range(1, planes):
        copies[step - 1].wait()
        total += chunk_in[step - 1]

    base = core * large + side * middle
    own = span(base + plane * small, small)
    out_ref[own, :] = total
    shift = 1 + planes
    copies = [
        put(out_ref.at[own], out_ref.at[own], shift + 1 + step, others[step - 1])
        for step in range(1, planes)
    ]
    for copy in copies:
        copy.wait()
    quarter = span(base, middle)
    put(out_ref.at[quarter], out_ref.at[quarter], shift + 1, other_side).wait()
    whole = span(core * large, large)
    put(out_ref.at[whole], out_ref.at[whole], shift, other_core).wait()


def reduced_gram(pair):
    width = pair.shape[1] // 2
    rows = 3 * width
    count = lax.axis_size("row")
    planes = count // 4
    vmem = pl.BlockSpec(memory_space=pltpu.VMEM)
    return pl.pallas_call(
        functools.partial(reduce_kernel, count),
        out_shape=jax.ShapeDtypeStruct((rows, width), jnp.float32),
        in_specs=[vmem],
        out_specs=vmem,
        scratch_shapes=[
            pltpu.VMEM((rows, width), jnp.float32),
            pltpu.VMEM((rows // 2, width), jnp.float32),
            pltpu.VMEM((rows // 2, width), jnp.float32),
            pltpu.VMEM((rows // 4, width), jnp.float32),
            pltpu.VMEM((rows // 4, width), jnp.float32),
            pltpu.VMEM((planes - 1, rows // count, width), jnp.float32),
            pltpu.SemaphoreType.DMA((2 + 2 * planes,)),
            pltpu.SemaphoreType.DMA((2 + 2 * planes,)),
        ],
        compiler_params=pltpu.CompilerParams(
            collective_id=0, has_side_effects=True, vmem_limit_bytes=32 << 20
        ),
    )(pair)


def body(matrix):
    width = matrix.shape[1] // 2
    col_place = lax.axis_index("col")
    col_last = lax.axis_size("col") - 1
    first_col = col_place == 0
    last_col = col_place == col_last
    top_block = matrix[:, :width]
    bottom_block = matrix[:, width:]
    pair_blocks = matrix[None]
    pair_gram = reduced_gram(pair_blocks[0])
    coupling_terms = []
    for step_index in range(STEPS):
        turn, local_term = rotation_of(pair_gram)
        coupling_terms.append(local_term)
        turned = jnp.einsum(
            "prk,lk->prl",
            pair_blocks,
            turn,
            precision=lax.Precision.HIGHEST,
            preferred_element_type=jnp.float32,
        )
        new_top = turned[0, :, :width]
        new_bottom = turned[0, :, width:]
        outgoing = jnp.where(first_col, new_bottom, new_top)
        arrived_top = from_behind(outgoing, "col", 1)
        arrived_bottom = from_behind(new_bottom, "col", -1)
        top_block = jnp.where(first_col, new_top, arrived_top)
        bottom_block = jnp.where(last_col, new_top, arrived_bottom)
        pair_blocks = jnp.concatenate([top_block, bottom_block], axis=1)[None]
        if step_index + 1 < STEPS:
            pair_gram = reduced_gram(pair_blocks[0])
    totals = lax.psum(jnp.stack(coupling_terms), "col")
    coupling = jnp.sqrt(totals / (1.0 * lax.axis_size("col") * width))
    rotated = jnp.concatenate([top_block, bottom_block], axis=1)
    return (rotated, coupling)


def solution(mesh):
    in_specs = (P("row", "col"),)
    out_specs = (P("row", "col"), P())
    return jax.shard_map(body, mesh=mesh, in_specs=in_specs, out_specs=out_specs, check_vma=False)
```

```python
import functools

import jax
import jax.numpy as jnp
from jax import lax
from jax.experimental import pallas as pl
from jax.experimental.pallas import tpu as pltpu
from jax.sharding import PartitionSpec as P

STEPS = 2


LEAF = 128
GROUP = 8
AHEAD = 4


def mat(left, right, contract):
    return lax.dot_general(
        left,
        right,
        (contract, ((), ())),
        precision=lax.Precision.HIGHEST,
        preferred_element_type=jnp.float32,
    )


def spread(row, shape):
    return jnp.broadcast_to(row, shape)


def inverse_factors(blocks):
    shape = (GROUP, LEAF)
    groups = LEAF // GROUP
    lane = lax.broadcasted_iota(jnp.int32, shape, 1)
    sub = lax.broadcasted_iota(jnp.int32, shape, 0)
    works = [[block[GROUP * i : GROUP * (i + 1), :] for i in range(groups)] for block in blocks]
    for start in range(0, LEAF, AHEAD):
        first = start // GROUP
        columns = [
            [
                [spread(work[i][:, start + t : start + t + 1], shape) for i in range(first, groups)]
                for t in range(AHEAD)
            ]
            for work in works
        ]
        for t in range(AHEAD):
            pivot = start + t
            inside = pivot % GROUP
            for work, column in zip(works, columns):
                own = column[t]
                scale = 1.0 / spread(own[0][inside : inside + 1, :], shape)
                for later in range(t + 1, AHEAD):
                    place = inside + later - t
                    factor = spread(own[0][place : place + 1, :], shape) * scale
                    column[later] = [c - o * factor for c, o in zip(column[later], own)]
                row = spread(work[first][inside : inside + 1, :], shape)
                here = lane == pivot
                row = jnp.where(here, 1.0, row) * scale
                for i in range(first, groups):
                    held = work[i]
                    if i == first:
                        below = sub > inside
                        updated = jnp.where(here, 0.0, held) - own[0] * row
                        work[i] = jnp.where(below, updated, held)
                    else:
                        work[i] = jnp.where(here, 0.0, held) - own[i - first] * row
    results = []
    for work in works:
        full = jnp.concatenate(work, axis=0)
        rows = lax.broadcasted_iota(jnp.int32, full.shape, 0)
        lanes = lax.broadcasted_iota(jnp.int32, full.shape, 1)
        pivots = jnp.sum(jnp.where(rows == lanes, full, 0.0), axis=1, keepdims=True)
        unit = jnp.where(rows == lanes, 1.0, jnp.where(rows > lanes, full, 0.0))
        results.append(unit * lax.rsqrt(pivots))
    return results


def rotation_kernel(gram_ref, turn_ref, term_ref, work, part, inner):
    half = gram_ref.shape[1]
    size = 2 * half
    count = size // LEAF
    same = lax.broadcasted_iota(jnp.int32, (half, half), 0) == lax.broadcasted_iota(
        jnp.int32, (half, half), 1
    )
    top, cross, bottom = (gram_ref[half * i : half * (i + 1), :] for i in range(3))
    down = jnp.sum(jnp.where(same, top, 0.0), axis=1, keepdims=True)
    across = jnp.sum(jnp.where(same, bottom, 0.0), axis=0, keepdims=True)
    total = jnp.sum(cross * cross / (down * across), axis=1, keepdims=True)
    total = jnp.sum(total, axis=0, keepdims=True)
    term_ref[...] = jnp.broadcast_to(total, term_ref.shape)

    eye = (
        lax.broadcasted_iota(jnp.int32, (LEAF, LEAF), 0)
        == lax.broadcasted_iota(jnp.int32, (LEAF, LEAF), 1)
    ).astype(jnp.float32)
    work[:half, :half] = top
    work[:half, half:] = cross
    work[half:, :half] = jnp.zeros_like(cross)
    work[half:, half:] = bottom
    turn_ref[...] = jnp.zeros_like(turn_ref)
    inner[...] = eye
    place_lanes = lax.broadcasted_iota(jnp.int32, (LEAF, size), 1)

    def stage(index, carry):
        now = jnp.minimum(index, count - 1)
        here = pl.ds(pl.multiple_of(now * LEAF, LEAF), LEAF)
        outer_inverse, inner_inverse = inverse_factors([work[here, here], inner[...]])

        @pl.when(index > 0)
        def _():
            before = pl.ds(pl.multiple_of((index - 1) * LEAF, LEAF), LEAF)
            turn_ref[before, :] = mat(inner_inverse, part[...], ((1,), (0,)))

        @pl.when(index < count)
        def _():
            factor = mat(outer_inverse, work[here, :], ((1,), (0,)))
            factor = jnp.where(place_lanes >= now * LEAF, factor, 0.0)
            turned = turn_ref[...]
            overlap = mat(factor, turned, ((1,), (1,)))
            rest = factor - mat(overlap, turned, ((1,), (0,)))
            part[...] = rest
            inner[...] = mat(rest, rest, ((1,), (1,)))
            work[...] -= mat(factor, factor, ((0,), (0,)))

        return carry

    lax.fori_loop(0, count + 1, stage, 0)


def rotation_of(pair_gram):
    size = 2 * pair_gram.shape[1]
    vmem = pl.BlockSpec(memory_space=pltpu.VMEM)
    turn, term = pl.pallas_call(
        rotation_kernel,
        out_shape=(
            jax.ShapeDtypeStruct((size, size), jnp.float32),
            jax.ShapeDtypeStruct((8, 128), jnp.float32),
        ),
        in_specs=[vmem],
        out_specs=(vmem, vmem),
        scratch_shapes=[
            pltpu.VMEM((size, size), jnp.float32),
            pltpu.VMEM((LEAF, size), jnp.float32),
            pltpu.VMEM((LEAF, LEAF), jnp.float32),
        ],
        compiler_params=pltpu.CompilerParams(vmem_limit_bytes=32 << 20),
    )(pair_gram)
    return turn, term


def reduce_kernel(count, pair_ref, out_ref, mine, half_in, half, part_in, part, chunk_in, send, recv):
    width = pair_ref.shape[1] // 2
    rows = out_ref.shape[0]
    planes = count // 4
    place = lax.axis_index("row")
    core = lax.rem(place, 2)
    side = lax.rem(place // 2, 2)
    plane = place // 4
    other_core = place + 1 - 2 * core
    other_side = place + 2 - 4 * side
    others = [4 * lax.rem(plane + step, planes) + 2 * side + core for step in range(1, planes)]

    barrier = pltpu.get_barrier_semaphore()
    for peer in [other_core, other_side] + others:
        pl.semaphore_signal(
            barrier, inc=1, device_id={"row": peer}, device_id_type=pl.DeviceIdType.MESH
        )

    top = pair_ref[:, :width]
    bottom = pair_ref[:, width:]
    mine[:width, :] = mat(top, top, ((0,), (0,)))
    mine[width : 2 * width, :] = mat(top, bottom, ((0,), (0,)))
    mine[2 * width :, :] = mat(bottom, bottom, ((0,), (0,)))
    pl.semaphore_wait(barrier, 1 + planes)

    def put(source, target, index, peer):
        copy = pltpu.make_async_remote_copy(
            src_ref=source,
            dst_ref=target,
            send_sem=send.at[index],
            recv_sem=recv.at[index],
            device_id={"row": peer},
            device_id_type=pl.DeviceIdType.MESH,
        )
        copy.start()
        return copy

    def span(start, length):
        return pl.ds(pl.multiple_of(start, 8), length)

    large, middle, small = rows // 2, rows // 4, rows // count
    put(mine.at[span((1 - core) * large, large)], half_in, 0, other_core).wait()
    half[...] = mine[span(core * large, large), :] + half_in[...]
    put(half.at[span((1 - side) * middle, middle)], part_in, 1, other_side).wait()
    part[...] = half[span(side * middle, middle), :] + part_in[...]
    copies = []
    for step in range(1, planes):
        there = lax.rem(plane + step, planes)
        source = part.at[span(there * small, small)]
        copies.append(put(source, chunk_in.at[step - 1], 1 + step, others[step - 1]))
    total = part[span(plane * small, small), :]
    for step in range(1, planes):
        copies[step - 1].wait()
        total += chunk_in[step - 1]

    base = core * large + side * middle
    own = span(base + plane * small, small)
    out_ref[own, :] = total
    shift = 1 + planes
    copies = [
        put(out_ref.at[own], out_ref.at[own], shift + 1 + step, others[step - 1])
        for step in range(1, planes)
    ]
    for copy in copies:
        copy.wait()
    quarter = span(base, middle)
    put(out_ref.at[quarter], out_ref.at[quarter], shift + 1, other_side).wait()
    whole = span(core * large, large)
    put(out_ref.at[whole], out_ref.at[whole], shift, other_core).wait()


def reduced_gram(pair):
    width = pair.shape[1] // 2
    rows = 3 * width
    count = lax.axis_size("row")
    planes = count // 4
    vmem = pl.BlockSpec(memory_space=pltpu.VMEM)
    return pl.pallas_call(
        functools.partial(reduce_kernel, count),
        out_shape=jax.ShapeDtypeStruct((rows, width), jnp.float32),
        in_specs=[vmem],
        out_specs=vmem,
        scratch_shapes=[
            pltpu.VMEM((rows, width), jnp.float32),
            pltpu.VMEM((rows // 2, width), jnp.float32),
            pltpu.VMEM((rows // 2, width), jnp.float32),
            pltpu.VMEM((rows // 4, width), jnp.float32),
            pltpu.VMEM((rows // 4, width), jnp.float32),
            pltpu.VMEM((planes - 1, rows // count, width), jnp.float32),
            pltpu.SemaphoreType.DMA((2 + 2 * planes,)),
            pltpu.SemaphoreType.DMA((2 + 2 * planes,)),
        ],
        compiler_params=pltpu.CompilerParams(
            collective_id=0, has_side_effects=True, vmem_limit_bytes=32 << 20
        ),
    )(pair)


def turn_kernel(count, pair_ref, turn_ref, terms_ref, out_ref, total_ref, leaving, shares, send, recv):
    width = pair_ref.shape[1] // 2
    place = lax.axis_index("col")
    last = count - 1
    peers = [lax.rem(place + step, count) for step in range(1, count)]
    left = pl.ds(0, width)
    right = pl.ds(width, width)

    barrier = pltpu.get_barrier_semaphore()
    for peer in peers:
        pl.semaphore_signal(
            barrier, inc=1, device_id={"col": peer}, device_id_type=pl.DeviceIdType.MESH
        )

    def put(source, target, index, peer):
        return pltpu.make_async_remote_copy(
            src_ref=source,
            dst_ref=target,
            send_sem=send.at[index],
            recv_sem=recv.at[index],
            device_id={"col": peer},
            device_id_type=pl.DeviceIdType.MESH,
        )

    leaving[1] = mat(pair_ref[...], turn_ref[width:, :], ((1,), (1,)))
    pl.semaphore_wait(barrier, count - 1)
    first_out = put(leaving.at[1], out_ref.at[:, left], 0, jnp.minimum(place + 1, last))
    top_out = put(leaving.at[0], out_ref.at[:, left], 0, jnp.minimum(place + 1, last))
    bottom_out = put(leaving.at[1], out_ref.at[:, right], 1, jnp.maximum(place - 1, 0))
    spread_out = [
        put(terms_ref, shares.at[place], 1 + step, peers[step - 1]) for step in range(1, count)
    ]

    @pl.when(place == 0)
    def _():
        first_out.start()

    @pl.when(place > 0)
    def _():
        bottom_out.start()

    for copy in spread_out:
        copy.start()

    leaving[0] = mat(pair_ref[...], turn_ref[:width, :], ((1,), (1,)))

    @pl.when(jnp.logical_and(place > 0, place < last))
    def _():
        top_out.start()

    @pl.when(place == 0)
    def _():
        out_ref[:, left] = leaving[0]

    @pl.when(place == last)
    def _():
        out_ref[:, right] = leaving[0]

    shares[place] = terms_ref[...]
    for copy in spread_out:
        copy.wait()
    total = shares[0]
    for step in range(1, count):
        total += shares[step]
    total_ref[...] = total

    @pl.when(place < last)
    def _():
        top_out.wait_send()
        bottom_out.wait_recv()

    @pl.when(place > 0)
    def _():
        bottom_out.wait_send()
        top_out.wait_recv()


def turned_pair(pair, turn, terms):
    width = pair.shape[1] // 2
    count = lax.axis_size("col")
    vmem = pl.BlockSpec(memory_space=pltpu.VMEM)
    return pl.pallas_call(
        functools.partial(turn_kernel, count),
        out_shape=(
            jax.ShapeDtypeStruct(pair.shape, jnp.float32),
            jax.ShapeDtypeStruct(terms.shape, jnp.float32),
        ),
        in_specs=[vmem, vmem, vmem],
        out_specs=(vmem, vmem),
        scratch_shapes=[
            pltpu.VMEM((2, pair.shape[0], width), jnp.float32),
            pltpu.VMEM((count,) + terms.shape, jnp.float32),
            pltpu.SemaphoreType.DMA((count + 1,)),
            pltpu.SemaphoreType.DMA((count + 1,)),
        ],
        compiler_params=pltpu.CompilerParams(
            collective_id=1, has_side_effects=True, vmem_limit_bytes=32 << 20
        ),
    )(pair, turn, terms)


def body(matrix):
    width = matrix.shape[1] // 2
    pair = matrix
    totals = []
    for _ in range(STEPS):
        turn, terms = rotation_of(reduced_gram(pair))
        pair, total = turned_pair(pair, turn, terms)
        totals.append(total[0, 0])
    coupling = jnp.sqrt(jnp.stack(totals) / (1.0 * lax.axis_size("col") * width))
    return (pair, coupling)


def solution(mesh):
    in_specs = (P("row", "col"),)
    out_specs = (P("row", "col"), P())
    return jax.shard_map(body, mesh=mesh, in_specs=in_specs, out_specs=out_specs, check_vma=False)
```
